512 devices in a mesh: dp: 16 (over z_lo, core), ctx: 32 (over y, x, z_hi).
Axes of the slice: x: 4, y: 4, z: 16 (z_hi: 2, z_lo: 8; z = z_hi * 8 + z_lo), core: 2. Of those that a mesh axis runs over, the one named last changes fastest.
Arguments:
- value: bfloat16 [16384, 8192], P('ctx', 'dp'), may hold values from -6 to 6
- gate: bfloat16 [16384, 8192], P('ctx', 'dp'), may hold values from -6 to 6
- grad_out: bfloat16 [16384, 8192], P('ctx', 'dp'), may hold values from -6 to 6
- filter_taps: float32 [16384, 32, 16], P('dp', 'ctx'), may hold values from -4 to 4
- skip: float32 [8192], P('dp'), may hold values from -3 to 3
Outputs:
- gate_grad: bfloat16 [16384, 8192], P('ctx', 'dp')
- filter_grad: float32 [16384, 32, 16], P('dp', 'ctx')
The draws below stay inside these ranges and needn't reach their ends.
All inputs are finite; a program needn't handle non-finite values.
Results may differ from the reference program's by a relative error of at most 0.012.
Values may be sent and summed in bfloat16 or wider, within the bound.
A program may use at most 64 MiB of HBM per device.

```python
import math
import jax
import jax.numpy as jnp
from jax import lax

C = 8192
GROUP = 16
L = 16384
GROUPS = 512
GPD = 32


def draw_filter_taps(key, part):
    key = jax.random.fold_in(key, 5)
    key_noise, key_rate = jax.random.split(key)
    blocks = GROUPS // GPD
    positions = jnp.arange(L, dtype=jnp.float32) / L
    noise = jnp.clip(jax.random.normal(key_noise, (L, GPD, blocks), jnp.float32), -4.0, 4.0)
    exponent = jax.random.uniform(key_rate, (GPD, blocks), jnp.float32, 0.0, 3.0)
    rates = 0.3 * jnp.exp(exponent * math.log(10.0))
    return noise * jnp.exp(-rates[None, :, :] * positions[:, None, None])


def shard_levels(own_key, dims, cuts, smallest, largest):
    factor_of, own = 1.0, jax.random.fold_in(own_key, 6)
    for axis_at, parts in cuts:
        heights = jnp.exp(jax.random.uniform(jax.random.fold_in(own, axis_at), (parts,), jnp.float32, smallest / len(cuts), largest / len(cuts)))
        factor_of = factor_of * jnp.repeat(heights, dims[axis_at] // parts).reshape([-1 if axis == axis_at else 1 for axis in range(len(dims))])
    return factor_of


def bell_draw(rng, dims, scale, bound, shards=(), kind=jnp.bfloat16):
    gain = shard_levels(rng, dims, shards, -0.22, 0.18) if shards else 1.0
    values = jax.random.normal(rng, dims, jnp.float32) * scale * gain
    return jnp.minimum(jnp.maximum(values, -bound), bound).astype(kind)


def setup_inputs(seed: int = 0) -> dict:
    seeds = jax.random.split(jax.random.key(seed), 6)
    return {
        "value": bell_draw(seeds[0], (L, C), 1.0, 6.0, ((0, 32), (1, 16))),
        "gate": bell_draw(seeds[1], (L, C), 1.0, 6.0, ((0, 32), (1, 16))),
        "grad_out": bell_draw(seeds[2], (L, C), 1.0, 6.0, ((0, 32), (1, 16))),
        "filter_taps": draw_filter_taps(jax.random.fold_in(seeds[5], 71), 0),
        "skip": bell_draw(seeds[4], (C,), 0.5, 3.0, ((0, 16),), jnp.float32),
    }


def reference(value, gate, grad_out, filter_taps, skip):
    length = value.shape[0]
    channels = value.shape[1]
    per_block_groups = filter_taps.shape[1]
    block_count = filter_taps.shape[2]
    groups = channels // GROUP
    padded_length = 2 * length
    taps = jnp.transpose(filter_taps, (0, 2, 1)).reshape(length, groups)
    filter_time = taps / jnp.sqrt(jnp.float32(length))
    group_spec = jnp.fft.rfft(filter_time, n=padded_length, axis=0)
    width = math.gcd(channels, 256)
    pieces = channels // width
    per_piece = width // GROUP
    spec_pieces = jnp.transpose(group_spec.reshape(length + 1, pieces, per_piece), (1, 0, 2))

    def split_cols(array):
        return jnp.transpose(array.reshape(length, pieces, width), (1, 0, 2))

    def one_piece(inputs):
        value_seq, gate_seq, cotangent, skip_piece, spec_piece = inputs
        channel_spec = jnp.repeat(spec_piece, GROUP, axis=1)
        value_wide = value_seq.astype(jnp.float32)
        value_spec = jnp.fft.rfft(value_wide, n=padded_length, axis=0)
        conv = jnp.fft.irfft(value_spec * channel_spec, n=padded_length, axis=0)[:length]
        long_out = (conv + skip_piece[None, :] * value_wide).astype(jnp.bfloat16)
        gate_grad = (cotangent.astype(jnp.float32) * long_out.astype(jnp.float32)).astype(jnp.bfloat16)
        gated = (gate_seq.astype(jnp.float32) * cotangent.astype(jnp.float32)).astype(jnp.bfloat16)
        gated_spec = jnp.fft.rfft(gated.astype(jnp.float32), n=padded_length, axis=0)
        corr = jnp.fft.irfft(gated_spec * jnp.conj(value_spec), n=padded_length, axis=0)[:length]
        grouped = lax.optimization_barrier(jnp.sum(corr.reshape(length, per_piece, GROUP), axis=2))
        return (gate_grad, grouped)
    skip_pieces = skip.reshape(pieces, width)
    grads, grouped = lax.map(one_piece, (split_cols(value), split_cols(gate), split_cols(grad_out), skip_pieces, spec_pieces))
    gate_grad = jnp.transpose(grads, (1, 0, 2)).reshape(length, channels)
    summed = jnp.transpose(grouped, (1, 0, 2)).reshape(length, groups)
    scaled = summed / jnp.sqrt(jnp.float32(length * GROUP))
    filter_grad = jnp.transpose(scaled.reshape(length, block_count, per_block_groups), (0, 2, 1))
    return (gate_grad, filter_grad)
```

```python
import functools

import jax
import jax.numpy as jnp
from jax import lax
from jax.experimental import pallas as pl
from jax.experimental.pallas import tpu as pltpu
from jax.sharding import PartitionSpec as P

MESH = pl.DeviceIdType.MESH
BF16 = jnp.bfloat16
F32 = jnp.float32

N_DP = 16
N_SLOT = 16
GROUP = 16
BLK = 512
T = 128
HALF = 256
PAD = 7
N_T = 128
COL = 32


def remote(src, dst, send, recv, device):
    return pltpu.make_async_remote_copy(
        src_ref=src, dst_ref=dst, send_sem=send, recv_sem=recv, device_id=device, device_id_type=MESH
    )


def loop(lower, upper, body):
    def step(i, carry):
        body(i)
        return carry

    lax.fori_loop(lower, upper, step, 0)


def kernel(
    value_hbm, gate_hbm, cot_hbm, taps_hbm, skip_hbm,
    out_ref, fg_ref,
    val, gat, cot, taps, skip,
    vloc, gloc, cot_t, tap_rows, taps_in, toep, vpad, gpad, vt, acc, lags, diag, lo, lo_in, fg, fg_in,
    in_sem, v_sem, g_sem, z_sem, tap_sem, lo_sem, fg_sem,
):
    dp = lax.axis_index("dp")
    ctx = lax.axis_index("ctx")
    side = lax.rem(ctx, 2)
    yx = ctx // 2
    col = dp * 2 + side

    def plane_peer(i):
        return lax.rem(yx + i, N_SLOT)

    def plane_device(i):
        return (dp, plane_peer(i) * 2 + side)

    def plane_source(i):
        return lax.rem(yx + N_SLOT - i, N_SLOT)

    def column_peer(r):
        return lax.rem(col + r, COL)

    def column_device(r):
        peer = column_peer(r)
        return (peer // 2, yx * 2 + lax.rem(peer, 2))

    def column_source(r):
        return lax.rem(col + COL - r, COL)

    partner = (dp, yx * 2 + 1 - side)

    barrier = pltpu.get_barrier_semaphore()
    loop(1, N_SLOT, lambda i: pl.semaphore_signal(barrier, inc=1, device_id=plane_device(i), device_id_type=MESH))
    loop(1, COL, lambda r: pl.semaphore_signal(barrier, inc=1, device_id=column_device(r), device_id_type=MESH))

    loads = [
        pltpu.make_async_copy(src, dst, in_sem.at[n])
        for n, (src, dst) in enumerate(
            ((value_hbm, val), (taps_hbm, taps), (cot_hbm, cot), (gate_hbm, gat), (skip_hbm, skip))
        )
    ]
    for load in loads:
        load.start()

    loads[0].wait()
    vloc[...] = val[...].T.reshape(N_SLOT, 2, GROUP, BLK)
    loads[1].wait()
    for c in range(8):
        tap_rows[:, c, :] = taps[:, c * T : (c + 1) * T]
    for g in range(2):
        for half in range(2):
            vpad[half, g, :HALF] = jnp.zeros((HALF, BLK), BF16)
        gpad[g, HALF:] = jnp.zeros((HALF, BLK), BF16)
        vpad[0, g, pl.ds(pl.multiple_of(HALF + yx * GROUP, GROUP), GROUP)] = vloc[yx, g]
        taps_own = taps_in.at[side, dp]
    taps_own[...] = tap_rows[dp]

    pl.semaphore_wait(barrier, N_SLOT - 1 + COL - 1)

    def v_copy(g, i, slot_at_receiver):
        return remote(
            vloc.at[plane_peer(i), g],
            vpad.at[0, g, pl.ds(pl.multiple_of(HALF + slot_at_receiver * GROUP, GROUP), GROUP)],
            v_sem.at[0, g, i], v_sem.at[1, g, i], plane_device(i),
        )

    def g_copy(g, i, slot_at_receiver):
        return remote(
            gloc.at[plane_peer(i), g],
            gpad.at[g, pl.ds(pl.multiple_of(slot_at_receiver * GROUP, GROUP), GROUP)],
            g_sem.at[0, g, i], g_sem.at[1, g, i], plane_device(i),
        )

    def z_copy(g, h, i):
        rows = pl.ds(pl.multiple_of(HALF + plane_source(i) * GROUP, GROUP), GROUP)
        cols = pl.ds(h * HALF, HALF)
        return remote(
            vpad.at[0, g, rows, cols], vpad.at[1, g, rows, cols],
            z_sem.at[0, g, h, i], z_sem.at[1, g, h, i], partner,
        )

    def tap_copy(r, half, row):
        return remote(
            tap_rows.at[column_peer(r) // 2], taps_in.at[half, row],
            tap_sem.at[0, r], tap_sem.at[1, r], column_device(r),
        )

    def lo_copy(g, i, slot_at_receiver):
        return remote(
            lo.at[g, pl.ds(pl.multiple_of(plane_peer(i) * GROUP, GROUP), GROUP)],
            lo_in.at[slot_at_receiver, g],
            lo_sem.at[0, g, i], lo_sem.at[1, g, i], plane_device(i),
        )

    def fg_copy(r, row, half):
        peer = column_peer(r)
        return remote(
            fg.at[lax.rem(peer, 2), peer // 2], fg_in.at[row, half],
            fg_sem.at[0, r], fg_sem.at[1, r], column_device(r),
        )

    loop(1, N_SLOT, lambda i: v_copy(0, i, yx).start())
    for h in range(2):
        z_copy(0, h, 0).start()
    loop(1, N_SLOT, lambda i: v_copy(1, i, yx).start())
    loop(1, COL, lambda r: tap_copy(r, side, dp).start())

    loads[2].wait()
    loads[3].wait()
    gloc[...] = (gat[...].astype(F32) * cot[...].astype(F32)).astype(BF16).T.reshape(N_SLOT, 2, GROUP, BLK)
    for g in range(2):
        loop(1, N_SLOT, lambda i, g=g: g_copy(g, i, yx).start())
        gpad[g, pl.ds(pl.multiple_of(yx * GROUP, GROUP), GROUP)] = gloc[yx, g]

    def pass_on(i):
        v_copy(0, i, plane_source(i)).wait_recv()
        z_copy(0, 0, i).start()

    loop(1, N_SLOT, pass_on)
    loop(1, N_SLOT, lambda i: z_copy(0, 1, i).start())

    cot_t[...] = cot[...].T.reshape(N_SLOT, 2, GROUP, BLK)

    rows_at = lax.broadcasted_iota(jnp.int32, (T, T), 0)
    lanes_at = lax.broadcasted_iota(jnp.int32, (T, T), 1)
    upper = lanes_at >= rows_at

    loop(1, COL, lambda r: tap_copy(r, lax.rem(column_source(r), 2), column_source(r) // 2).wait_recv())
    for g in range(2):
        toep[g, :PAD] = jnp.zeros((PAD, T, T), BF16)

        def build(d, before, g=g):
            for c in range(8):
                row = taps_in[g, d, c : c + 1, :]
                turned = pltpu.roll(jnp.broadcast_to(row, (T, T)), 0, 1, stride=1, stride_axis=0)
                toep[g, PAD + d * 8 + c] = jnp.where(upper, turned, before).astype(BF16)
                before = turned
            return before

        lax.fori_loop(0, N_DP, build, jnp.zeros((T, T), F32))

        def clear(n, g=g):
            lags[g, n] = jnp.zeros((T, T), F32)

        loop(0, N_T + PAD + 1, clear)
        acc[g] = jnp.zeros((HALF, BLK), F32)

    def lag_of(half, d):
        return 2 * d if half == 0 else 2 * d + 2 * side - 1

    def convolve(half, g, hs):
        lanes = slice(hs[0] * HALF, (hs[-1] + 1) * HALF)

        def step(d):
            k = lag_of(half, d)
            left = vpad[half, g, pl.ds(pl.multiple_of((N_SLOT - d) * GROUP, GROUP), HALF), lanes]
            us = [2 * h + e for h in hs for e in range(2)]
            tiles = {n: toep[g, 4 * k + n + PAD] for n in range(-us[-1], 4 - us[0])}
            right = jnp.concatenate(
                [jnp.concatenate([tiles[v - u] for v in range(4)], axis=1) for u in us], axis=0
            )
            acc[g] += jnp.dot(left, right, preferred_element_type=F32)

        loop(0, N_SLOT, step)

    def correlate(half, g, hs):
        lanes = slice(hs[0] * HALF, (hs[-1] + 1) * HALF)
        depth = HALF * len(hs)
        vt[:depth] = vpad[half, g, HALF:, lanes].T

        def step(d):
            k = lag_of(half, d)
            right = gpad[g, pl.ds(pl.multiple_of(d * GROUP, GROUP), HALF), :]
            product = jnp.dot(vt[:depth], right, preferred_element_type=F32)
            ws = [2 * h + e for h in hs for e in range(2)]
            for n in range(-ws[-1], 4 - ws[0]):
                terms = [
                    product[at * T : (at + 1) * T, (w + n) * T : (w + n + 1) * T]
                    for at, w in enumerate(ws)
                    if 0 <= w + n < 4
                ]
                lags[g, 4 * k + n + PAD] += functools.reduce(lambda a, b: a + b, terms)

        loop(0, N_SLOT, step)

    def finish_conv(g):
        scale = skip[pl.ds(pl.multiple_of(yx * 2 * GROUP + g * GROUP, GROUP), GROUP), :]
        scale = jnp.broadcast_to(scale[:, None, :], (GROUP, 4, T)).reshape(GROUP, BLK)

        def piece(n):
            rows = pl.ds(pl.multiple_of(n * GROUP, GROUP), GROUP)
            wide = vpad[0, g, pl.ds(pl.multiple_of(HALF + n * GROUP, GROUP), GROUP), :].astype(F32)
            lo[g, rows, :] = (acc[g, rows, :] * (1.0 / 128.0) + scale * wide).astype(BF16)

        loop(0, N_SLOT, piece)
        loop(1, N_SLOT, lambda i: lo_copy(g, i, yx).start())
        lo_in[yx, g] = lo[g, pl.ds(pl.multiple_of(yx * GROUP, GROUP), GROUP), :]

    def finish_corr(g):
        def strip(d):
            for c in range(8):
                at = PAD + d * 8 + c
                mixed = jnp.where(upper, lags[g, at], lags[g, at + 1])
                diag[d * 8 + c] = functools.reduce(
                    lambda a, b: a + b,
                    [pltpu.roll(mixed[q : q + 8], (T - q) % T, 1) for q in range(0, T, 8)],
                )

        loop(0, N_DP, strip)
        total = functools.reduce(
            lambda a, b: a + b, [pltpu.roll(diag[:, q, :], (T - q) % T, 1) for q in range(8)]
        )
        fg[g] = total.reshape(N_DP, 8, T)

        def send(r):
            @pl.when(lax.rem(column_peer(r), 2) == g)
            def _():
                fg_copy(r, dp, side).start()

        loop(1, COL, send)

    def gate_grad(g):
        loop(1, N_SLOT, lambda i: lo_copy(g, i, plane_source(i)).wait_recv())

        def piece(n):
            wide = lo_in[n, g].astype(F32) * cot_t[n, g].astype(F32)
            out_ref[pl.ds(pl.multiple_of(n * 2 * GROUP + g * GROUP, GROUP), GROUP), :] = wide.astype(BF16)

        loop(0, N_SLOT, piece)

    for g in range(2):
        loop(1, N_SLOT, lambda i, g=g: g_copy(g, i, plane_source(i)).wait_recv())
        if g == 1:
            loop(1, N_SLOT, lambda i: v_copy(1, i, plane_source(i)).wait_recv())
            for h in range(2):
                loop(0, N_SLOT, lambda i, h=h: z_copy(1, h, i).start())
        convolve(0, g, (0, 1))
        correlate(0, g, (0, 1))

    loads[4].wait()
    for g in range(2):
        for h in range(2):
            loop(0, N_SLOT, lambda i, g=g, h=h: z_copy(g, h, i).wait_recv())
            convolve(1, g, (h,))
            if h == 1:
                finish_conv(g)
            correlate(1, g, (h,))
        finish_corr(g)
        if g == 0:
            gate_grad(0)

    gate_grad(1)
    loop(1, COL, lambda r: fg_copy(r, column_source(r) // 2, lax.rem(column_source(r), 2)).wait_recv())
    fg_in[dp, side] = fg[side, dp]
    for c in range(8):
        fg_ref[:, c * T : (c + 1) * T] = (fg_in[:, 0, c, :] + fg_in[:, 1, c, :]) * (1.0 / 512.0)

    for g in range(2):

        def sent(i, g=g):
            v_copy(g, i, yx).wait_send()
            g_copy(g, i, yx).wait_send()
            lo_copy(g, i, yx).wait_send()

        loop(1, N_SLOT, sent)
        for h in range(2):
            loop(0, N_SLOT, lambda i, g=g, h=h: z_copy(g, h, i).wait_send())

    def sent_column(r):
        tap_copy(r, side, dp).wait_send()
        fg_copy(r, dp, side).wait_send()

    loop(1, COL, sent_column)


def shards(value, gate, grad_out, filter_taps, skip):
    taps = filter_taps[:, 0, :].T
    skip_wide = jnp.broadcast_to(skip[:, None], (BLK, T))
    any_spec = pl.BlockSpec(memory_space=pl.ANY)
    vmem_spec = pl.BlockSpec(memory_space=pltpu.VMEM)
    grad_t, fg = pl.pallas_call(
        kernel,
        out_shape=(
            jax.ShapeDtypeStruct((BLK, BLK), BF16),
            jax.ShapeDtypeStruct((N_DP, 1024), F32),
        ),
        in_specs=[any_spec] * 5,
        out_specs=(vmem_spec, vmem_spec),
        scratch_shapes=[
            pltpu.VMEM((BLK, BLK), BF16),
            pltpu.VMEM((BLK, BLK), BF16),
            pltpu.VMEM((BLK, BLK), BF16),
            pltpu.VMEM((N_DP, 1024), F32),
            pltpu.VMEM((BLK, T), F32),
            pltpu.VMEM((N_SLOT, 2, GROUP, BLK), BF16),
            pltpu.VMEM((N_SLOT, 2, GROUP, BLK), BF16),
            pltpu.VMEM((N_SLOT, 2, GROUP, BLK), BF16),
            pltpu.VMEM((N_DP, 8, T), F32),
            pltpu.VMEM((2, N_DP, 8, T), F32),
            pltpu.VMEM((2, N_T + PAD, T, T), BF16),
            pltpu.VMEM((2, 2, BLK, BLK), BF16),
            pltpu.VMEM((2, BLK, BLK), BF16),
            pltpu.VMEM((BLK, HALF), BF16),
            pltpu.VMEM((2, HALF, BLK), F32),
            pltpu.VMEM((2, N_T + PAD + 1, T, T), F32),
            pltpu.VMEM((N_T, 8, T), F32),
            pltpu.VMEM((2, HALF, BLK), BF16),
            pltpu.VMEM((N_SLOT, 2, GROUP, BLK), BF16),
            pltpu.VMEM((2, N_DP, 8, T), F32),
            pltpu.VMEM((N_DP, 2, 8, T), F32),
            pltpu.SemaphoreType.DMA((5,)),
            pltpu.SemaphoreType.DMA((2, 2, N_SLOT)),
            pltpu.SemaphoreType.DMA((2, 2, N_SLOT)),
            pltpu.SemaphoreType.DMA((2, 2, 2, N_SLOT)),
            pltpu.SemaphoreType.DMA((2, COL)),
            pltpu.SemaphoreType.DMA((2, 2, N_SLOT)),
            pltpu.SemaphoreType.DMA((2, COL)),
        ],
        compiler_params=pltpu.CompilerParams(
            collective_id=0, has_side_effects=True, vmem_limit_bytes=56 * 2**20
        ),
        cost_estimate=pl.CostEstimate(flops=2 * 2**33, bytes_accessed=4 * 2**20, transcendentals=0),
        name="hyena",
    )(value, gate, grad_out, taps, skip_wide)
    return grad_t.T, fg.T[:, None, :]


def solution(mesh):
    in_specs = (P("ctx", "dp"), P("ctx", "dp"), P("ctx", "dp"), P("dp", "ctx", None), P("dp"))
    out_specs = (P("ctx", "dp"), P("dp", "ctx", None))
    return jax.shard_map(shards, mesh=mesh, in_specs=in_specs, out_specs=out_specs, check_vma=False)
```

```python
import functools

import jax
import jax.numpy as jnp
from jax import lax
from jax.experimental import pallas as pl
from jax.experimental.pallas import tpu as pltpu
from jax.sharding import PartitionSpec as P

MESH = pl.DeviceIdType.MESH
BF16 = jnp.bfloat16
F32 = jnp.float32

N_DP = 16
N_SLOT = 16
GROUP = 16
BLK = 512
T = 128
HALF = 256
PAD = 7
N_T = 128
PILE = 16


def remote(src, dst, send, recv, device):
    return pltpu.make_async_remote_copy(
        src_ref=src, dst_ref=dst, send_sem=send, recv_sem=recv, device_id=device, device_id_type=MESH
    )


def loop(lower, upper, body):
    def step(i, carry):
        body(i)
        return carry

    lax.fori_loop(lower, upper, step, 0)


def kernel(
    value_hbm, gate_hbm, cot_hbm, taps_hbm, skip_hbm,
    out_ref, fg_ref,
    val, gat, cot, taps, skip, skip_rows,
    vloc, gloc, tap_own, tap_sib, tap_mix, taps_in, toep, relay, vals, gpad, acc, lags, diag, lo, lo_in,
    fg, fg_in, fg_own, fg_sib, fg_rows,
    in_sem, v_sem, g_sem, r_sem, z_sem, tap_sem, lo_sem, fg_sem, sib_sem,
):
    dp = lax.axis_index("dp")
    ctx = lax.axis_index("ctx")
    core = lax.rem(dp, 2)
    side = lax.rem(ctx, 2)
    yx = ctx // 2
    z = side * 8 + dp // 2
    z_lo = dp // 2
    pile = z_lo * 2 + side
    sibling = (dp + 1 - 2 * core, ctx)

    def device(z_at, yx_at):
        z_at = lax.rem(z_at + 16, 16)
        return (lax.rem(z_at, 8) * 2 + core, yx_at * 2 + z_at // 8)

    def plane_peer(i):
        return lax.rem(yx + i, N_SLOT)

    def plane_device(i):
        return (dp, plane_peer(i) * 2 + side)

    def plane_source(i):
        return lax.rem(yx + N_SLOT - i, N_SLOT)

    def pile_peer(r):
        return lax.rem(pile + r, PILE)

    def pile_device(r):
        peer = pile_peer(r)
        return (peer // 2 * 2 + core, yx * 2 + lax.rem(peer, 2))

    def pile_source(r):
        return lax.rem(pile + PILE - r, PILE)

    def way(i):
        return 1 - 2 * lax.rem(i, 2)

    def rows_at(slot):
        return pl.ds(pl.multiple_of(slot * GROUP, GROUP), GROUP)

    barrier = pltpu.get_barrier_semaphore()

    def greet(target):
        pl.semaphore_signal(barrier, inc=1, device_id=target, device_id_type=MESH)

    loop(1, PILE, lambda r: greet(pile_device(r)))
    greet(sibling)
    loop(1, N_SLOT, lambda i: greet(device(z - way(i), plane_source(i))))
    loop(1, N_SLOT, lambda i: greet(plane_device(i)))

    loads = [
        pltpu.make_async_copy(src, dst, in_sem.at[n])
        for n, (src, dst) in enumerate(
            ((value_hbm, val), (taps_hbm, taps), (cot_hbm, cot), (gate_hbm, gat), (skip_hbm, skip))
        )
    ]
    for load in loads:
        load.start()

    loads[0].wait()
    vloc[...] = val[...].T.reshape(N_SLOT, 2, GROUP, BLK)
    loads[1].wait()
    for b in range(N_DP):
        for c in range(8):
            tap_own[b % 2, b // 2, c : c + 1, :] = taps[b : b + 1, c * T : (c + 1) * T]
    for g in range(2):
        gpad[g, HALF:] = jnp.zeros((HALF, BLK), BF16)
        vals[0, g, rows_at(yx)] = vloc[yx, g]

    pl.semaphore_wait(barrier, PILE + 2 * (N_SLOT - 1))

    def r_copy(g, i, slot_at_receiver):
        return remote(
            vloc.at[plane_peer(i), g], relay.at[g, rows_at(slot_at_receiver)],
            r_sem.at[0, g, i], r_sem.at[1, g, i], device(z + way(i), plane_peer(i)),
        )

    def z_copy(g, h, i):
        lanes = pl.ds(pl.multiple_of(h * HALF, HALF), HALF)
        slot = plane_source(i)
        return remote(
            relay.at[g, rows_at(slot), lanes], vals.at[1, g, rows_at(slot), lanes],
            z_sem.at[0, g, h, i], z_sem.at[1, g, h, i], device(z + 7 * way(i), yx),
        )

    def v_copy(g, i, slot_at_receiver):
        return remote(
            vloc.at[plane_peer(i), g], vals.at[0, g, rows_at(slot_at_receiver)],
            v_sem.at[0, g, i], v_sem.at[1, g, i], plane_device(i),
        )

    def g_copy(g, i, slot_at_receiver):
        return remote(
            gloc.at[plane_peer(i), g], gpad.at[g, rows_at(slot_at_receiver)],
            g_sem.at[0, g, i], g_sem.at[1, g, i], plane_device(i),
        )

    tap_trade = remote(tap_own.at[1 - core], tap_sib, sib_sem.at[0, 0], sib_sem.at[1, 0], sibling)
    fg_trade = remote(fg_own.at[1 - core], fg_sib, sib_sem.at[0, 1], sib_sem.at[1, 1], sibling)

    def tap_copy(r, half, row):
        return remote(
            tap_mix.at[pile_peer(r) // 2], taps_in.at[half, row],
            tap_sem.at[0, r], tap_sem.at[1, r], pile_device(r),
        )

    def lo_copy(g, i, slot_at_receiver):
        return remote(
            lo.at[g, rows_at(plane_peer(i))], lo_in.at[slot_at_receiver, g],
            lo_sem.at[0, g, i], lo_sem.at[1, g, i], plane_device(i),
        )

    def fg_copy(r, row, half):
        peer = pile_peer(r)
        return remote(
            fg.at[lax.rem(peer, 2), peer // 2], fg_in.at[row, half],
            fg_sem.at[0, r], fg_sem.at[1, r], pile_device(r),
        )

    tap_trade.start()
    for g in range(2):
        loop(0, N_SLOT, lambda i, g=g: r_copy(g, i, yx).start())
    loop(1, N_SLOT, lambda i: v_copy(0, i, yx).start())
    tap_trade.wait_recv()
    mine, other = tap_own[core], tap_sib[...]
    tap_mix[...] = jnp.concatenate(
        [jnp.where(core == 0, mine, other), jnp.where(core == 0, other, mine)], axis=1
    ).astype(BF16)
    loop(1, PILE, lambda r: tap_copy(r, side, z_lo).start())
    taps_in[side, z_lo] = tap_mix[z_lo]
    loop(1, N_SLOT, lambda i: v_copy(1, i, yx).start())

    loads[2].wait()
    loads[3].wait()
    gloc[...] = (gat[...].astype(F32) * cot[...].astype(F32)).astype(BF16).T.reshape(N_SLOT, 2, GROUP, BLK)
    for g in range(2):
        loop(1, N_SLOT, lambda i, g=g: g_copy(g, i, yx).start())
        gpad[g, rows_at(yx)] = gloc[yx, g]

    def pass_on(i):
        r_copy(0, i, plane_source(i)).wait_recv()
        z_copy(0, 0, i).start()

    loop(0, N_SLOT, pass_on)
    loop(0, N_SLOT, lambda i: z_copy(0, 1, i).start())

    loads[4].wait()
    skip_rows[...] = jnp.broadcast_to(skip[...], (T, BLK)).T

    q_at = lax.broadcasted_iota(jnp.int32, (T, T), 0)
    p_at = lax.broadcasted_iota(jnp.int32, (T, T), 1)
    upper = p_at >= q_at

    for g in range(2):
        toep[g, :PAD] = jnp.zeros((PAD, T, T), BF16)
        for n in [0, 1, 2] + list(range(3, N_T + PAD, 8)) + list(range(N_T + 4, N_T + PAD + 1)):
            lags[g, n] = jnp.zeros((T, T), F32)

    loop(1, PILE, lambda r: tap_copy(r, lax.rem(pile_source(r), 2), pile_source(r) // 2).wait_recv())
    for g in range(2):

        def build(d, before, g=g):
            rows = taps_in[g, d].astype(F32)
            for c in range(16):
                turned = pltpu.roll(jnp.broadcast_to(rows[c : c + 1], (T, T)), 0, 1, stride=1, stride_axis=0)
                toep[g, PAD + d * 16 + c] = jnp.where(upper, turned, before).astype(BF16)
                before = turned
            return before

        lax.fori_loop(0, 8, build, jnp.zeros((T, T), F32))

    def convolve(half, g, h, width):
        lanes = pl.ds(pl.multiple_of(h * HALF, HALF), width * HALF)
        for d in range(N_SLOT):
            base = 8 * d + PAD if half == 0 else 8 * d + 8 * side - 4 - 2 * h + PAD
            left = vals[half, g, : HALF - d * GROUP, lanes]
            tiles = {n: toep[g, base + n] for n in range(1 - 2 * width, 4)}
            right = jnp.concatenate(
                [jnp.concatenate([tiles[v - u] for v in range(4)], axis=1) for u in range(2 * width)], axis=0
            )
            product = jnp.dot(left, right, preferred_element_type=F32)
            if half == 0 and d == 0:
                acc[g] = product
            else:
                acc[g, d * GROUP :] += product

    def correlate(half, g, h, width):
        lanes = pl.ds(pl.multiple_of(h * HALF, HALF), width * HALF)
        left = vals[half, g, :, lanes].T
        for d in range(N_SLOT):
            base = 8 * d + PAD if half == 0 else 8 * d + 8 * side - 4 - 2 * h + PAD
            right = gpad[g, d * GROUP : d * GROUP + HALF, :]
            product = jnp.dot(left, right, preferred_element_type=F32)
            for n in range(1 - 2 * width, 4):
                part = functools.reduce(
                    lambda a, b: a + b,
                    [
                        product[w * T : (w + 1) * T, (w + n) * T : (w + n + 1) * T]
                        for w in range(2 * width)
                        if 0 <= w + n < 4
                    ],
                )
                if half == 0:
                    lags[g, base + n] = part
                else:
                    lags[g, base + n] += part

    def finish_conv(g):
        scale = skip_rows[pl.ds(pl.multiple_of((yx * 2 + g) * GROUP, GROUP), GROUP), :]
        scale = jnp.concatenate([scale] * 4, axis=1)
        for n in range(N_SLOT):
            wide = vals[0, g, n * GROUP : (n + 1) * GROUP, :].astype(F32)
            rows = slice(n * GROUP, (n + 1) * GROUP)
            lo[g, rows, :] = (acc[g, rows, :] * (1.0 / 128.0) + scale * wide).astype(BF16)
        loop(1, N_SLOT, lambda i: lo_copy(g, i, yx).start())
        lo_in[yx, g] = lo[g, rows_at(yx), :]

    def finish_corr(g):
        def strip(d):
            for c in range(8):
                at = PAD + d * 8 + c
                mixed = jnp.where(upper, lags[g, at], lags[g, at + 1])
                diag[d * 8 + c] = functools.reduce(
                    lambda a, b: a + b,
                    [pltpu.roll(mixed[q : q + 8], (T - q) % T, 1) for q in range(0, T, 8)],
                )

        loop(0, N_DP, strip)
        total = functools.reduce(
            lambda a, b: a + b, [pltpu.roll(diag[:, q, :], (T - q) % T, 1) for q in range(8)]
        )
        fg[g] = total.reshape(8, 16, T).astype(BF16)

        def send(r):
            @pl.when(lax.rem(pile_peer(r), 2) == g)
            def _():
                fg_copy(r, z_lo, side).start()

        loop(1, PILE, send)

    loop(0, N_SLOT, lambda i: r_copy(1, i, plane_source(i)).wait_recv())
    for g in range(2):

        def arrived(i, g=g):
            v_copy(g, i, plane_source(i)).wait_recv()
            g_copy(g, i, plane_source(i)).wait_recv()

        loop(1, N_SLOT, arrived)

    def own(g):
        convolve(0, g, 0, 2)
        correlate(0, g, 0, 2)

    loop(0, 2, own)

    def phase(n):
        g = n // 2
        h = lax.rem(n, 2)
        loop(0, N_SLOT, lambda i: z_copy(g, h, i).wait_recv())

        @pl.when(g == 0)
        def _():
            loop(0, N_SLOT, lambda i: z_copy(1, h, i).start())

        convolve(1, g, h, 1)

        @pl.when(h == 1)
        def _():
            finish_conv(g)

        correlate(1, g, h, 1)

        @pl.when(h == 1)
        def _():
            finish_corr(g)

    loop(0, 4, phase)

    for g in range(2):
        loop(1, N_SLOT, lambda i, g=g: lo_copy(g, i, plane_source(i)).wait_recv())
    long_out = lo_in[...].reshape(BLK, BLK).T
    out_ref[...] = (long_out.astype(F32) * cot[...].astype(F32)).astype(BF16)

    loop(1, PILE, lambda r: fg_copy(r, pile_source(r) // 2, lax.rem(pile_source(r), 2)).wait_recv())
    fg_in[z_lo, side] = fg[side, z_lo]
    both = (fg_in[:, 0].astype(F32) + fg_in[:, 1].astype(F32)) * (1.0 / 512.0)
    fg_own[0] = both[:, :8]
    fg_own[1] = both[:, 8:]
    fg_trade.start()
    fg_trade.wait_recv()
    mine, other = fg_own[core], fg_sib[...]
    fg_rows[:, 0] = jnp.where(core == 0, mine, other)
    fg_rows[:, 1] = jnp.where(core == 0, other, mine)
    for b in range(N_DP):
        for c in range(8):
            fg_ref[b : b + 1, c * T : (c + 1) * T] = fg_rows[b // 2, b % 2, c : c + 1, :]

    tap_trade.wait_send()
    fg_trade.wait_send()
    for g in range(2):

        def sent(i, g=g):
            v_copy(g, i, yx).wait_send()
            g_copy(g, i, yx).wait_send()
            lo_copy(g, i, yx).wait_send()

        loop(1, N_SLOT, sent)

        def sent_over(i, g=g):
            r_copy(g, i, yx).wait_send()
            for h in range(2):
                z_copy(g, h, i).wait_send()

        loop(0, N_SLOT, sent_over)

    def sent_column(r):
        tap_copy(r, side, z_lo).wait_send()
        fg_copy(r, z_lo, side).wait_send()

    loop(1, PILE, sent_column)


def shards(value, gate, grad_out, filter_taps, skip):
    taps = filter_taps[:, 0, :].T
    any_spec = pl.BlockSpec(memory_space=pl.ANY)
    vmem_spec = pl.BlockSpec(memory_space=pltpu.VMEM)
    grad, fg = pl.pallas_call(
        kernel,
        out_shape=(
            jax.ShapeDtypeStruct((BLK, BLK), BF16),
            jax.ShapeDtypeStruct((N_DP, 1024), F32),
        ),
        in_specs=[any_spec] * 5,
        out_specs=(vmem_spec, vmem_spec),
        scratch_shapes=[
            pltpu.VMEM((BLK, BLK), BF16),
            pltpu.VMEM((BLK, BLK), BF16),
            pltpu.VMEM((BLK, BLK), BF16),
            pltpu.VMEM((N_DP, 1024), F32),
            pltpu.VMEM((1, BLK), F32),
            pltpu.VMEM((BLK, T), F32),
            pltpu.VMEM((N_SLOT, 2, GROUP, BLK), BF16),
            pltpu.VMEM((N_SLOT, 2, GROUP, BLK), BF16),
            pltpu.VMEM((2, 8, 8, T), F32),
            pltpu.VMEM((8, 8, T), F32),
            pltpu.VMEM((8, 16, T), BF16),
            pltpu.VMEM((2, 8, 16, T), BF16),
            pltpu.VMEM((2, N_T + PAD, T, T), BF16),
            pltpu.VMEM((2, HALF, BLK), BF16),
            pltpu.VMEM((2, 2, HALF, BLK), BF16),
            pltpu.VMEM((2, BLK, BLK), BF16),
            pltpu.VMEM((2, HALF, BLK), F32),
            pltpu.VMEM((2, N_T + PAD + 1, T, T), F32),
            pltpu.VMEM((N_T, 8, T), F32),
            pltpu.VMEM((2, HALF, BLK), BF16),
            pltpu.VMEM((N_SLOT, 2, GROUP, BLK), BF16),
            pltpu.VMEM((2, 8, 16, T), BF16),
            pltpu.VMEM((8, 2, 16, T), BF16),
            pltpu.VMEM((2, 8, 8, T), F32),
            pltpu.VMEM((8, 8, T), F32),
            pltpu.VMEM((8, 2, 8, T), F32),
            pltpu.SemaphoreType.DMA((5,)),
            pltpu.SemaphoreType.DMA((2, 2, N_SLOT)),
            pltpu.SemaphoreType.DMA((2, 2, N_SLOT)),
            pltpu.SemaphoreType.DMA((2, 2, N_SLOT)),
            pltpu.SemaphoreType.DMA((2, 2, 2, N_SLOT)),
            pltpu.SemaphoreType.DMA((2, PILE)),
            pltpu.SemaphoreType.DMA((2, 2, N_SLOT)),
            pltpu.SemaphoreType.DMA((2, PILE)),
            pltpu.SemaphoreType.DMA((2, 2)),
        ],
        compiler_params=pltpu.CompilerParams(
            collective_id=0, has_side_effects=True, vmem_limit_bytes=56 * 2**20
        ),
        cost_estimate=pl.CostEstimate(flops=2 * 2**33, bytes_accessed=4 * 2**20, transcendentals=0),
        name="hyena",
    )(value, gate, grad_out, taps, skip[None, :])
    return grad, fg.T[:, None, :]


def solution(mesh):
    in_specs = (P("ctx", "dp"), P("ctx", "dp"), P("ctx", "dp"), P("dp", "ctx", None), P("dp"))
    out_specs = (P("ctx", "dp"), P("dp", "ctx", None))
    return jax.shard_map(shards, mesh=mesh, in_specs=in_specs, out_specs=out_specs, check_vma=False)
```

```python
import functools

import jax
import jax.numpy as jnp
from jax import lax
from jax.experimental import pallas as pl
from jax.experimental.pallas import tpu as pltpu
from jax.sharding import PartitionSpec as P

MESH = pl.DeviceIdType.MESH
BF16 = jnp.bfloat16
F32 = jnp.float32

N_DP = 16
N_SLOT = 16
GROUP = 16
BLK = 512
T = 128
HALF = 256
PAD = 7
N_T = 128
PILE = 16


def remote(src, dst, send, recv, device):
    return pltpu.make_async_remote_copy(
        src_ref=src, dst_ref=dst, send_sem=send, recv_sem=recv, device_id=device, device_id_type=MESH
    )


def loop(lower, upper, body, unroll=True):
    def step(i, carry):
        body(i)
        return carry

    if upper - lower in (15, 16) and unroll:
        for i in range(lower, upper):
            body(i)
        return
    lax.fori_loop(lower, upper, step, 0)


def kernel(
    value_hbm, gate_hbm, cot_hbm, taps_hbm, skip_hbm,
    out_ref, fg_ref,
    val, gat, cot, taps, skip, skip_rows,
    vloc, gloc, tap_own, tap_sib, tap_mix, taps_in, toep, relay, vals, gpad, acc, lags, diag, lo, lo_in,
    fg, fg_in, fg_own, fg_sib, fg_rows,
    in_sem, v_sem, g_sem, r_sem, z_sem, tap_sem, lo_sem, fg_sem, sib_sem,
):
    dp = lax.axis_index("dp")
    ctx = lax.axis_index("ctx")
    core = lax.rem(dp, 2)
    side = lax.rem(ctx, 2)
    yx = ctx // 2
    z = side * 8 + dp // 2
    z_lo = dp // 2
    pile = z_lo * 2 + side
    sibling = (dp + 1 - 2 * core, ctx)

    def device(z_at, yx_at):
        z_at = lax.rem(z_at + 16, 16)
        return (lax.rem(z_at, 8) * 2 + core, yx_at * 2 + z_at // 8)

    def plane_peer(i):
        return lax.rem(yx + i, N_SLOT)

    def plane_device(i):
        return (dp, plane_peer(i) * 2 + side)

    def plane_source(i):
        return lax.rem(yx + N_SLOT - i, N_SLOT)

    def pile_peer(r):
        return lax.rem(pile + r, PILE)

    def pile_device(r):
        peer = pile_peer(r)
        return (peer // 2 * 2 + core, yx * 2 + lax.rem(peer, 2))

    def pile_source(r):
        return lax.rem(pile + PILE - r, PILE)

    def way(one, two):
        return 1 - 2 * lax.rem(one // 8 + two // 8, 2)

    def rows_at(slot):
        return pl.ds(pl.multiple_of(slot * GROUP, GROUP), GROUP)

    barrier = pltpu.get_barrier_semaphore()

    def greet(target):
        pl.semaphore_signal(barrier, inc=1, device_id=target, device_id_type=MESH)

    loop(1, PILE, lambda r: greet(pile_device(r)))
    greet(sibling)
    loop(1, N_SLOT, lambda i: greet(device(z - way(plane_source(i), yx), plane_source(i))))
    loop(1, N_SLOT, lambda i: greet(plane_device(i)))

    loads = [
        pltpu.make_async_copy(src, dst, in_sem.at[n])
        for n, (src, dst) in enumerate(
            ((value_hbm, val), (taps_hbm, taps), (cot_hbm, cot), (gate_hbm, gat), (skip_hbm, skip))
        )
    ]
    for load in loads:
        load.start()

    loads[0].wait()
    vloc[...] = val[...].T.reshape(N_SLOT, 2, GROUP, BLK)
    loads[1].wait()
    for b in range(N_DP):
        for c in range(8):
            tap_own[b % 2, b // 2, c : c + 1, :] = taps[b : b + 1, c * T : (c + 1) * T]
    loads[2].wait()
    loads[3].wait()
    gloc[...] = (gat[...].astype(F32) * cot[...].astype(F32)).astype(BF16).T.reshape(N_SLOT, 2, GROUP, BLK)

    pl.semaphore_wait(barrier, PILE + 2 * (N_SLOT - 1))

    def r_copy(i, slot_at_receiver):
        return remote(
            vloc.at[plane_peer(i)], relay.at[:, rows_at(slot_at_receiver)],
            r_sem.at[0, i], r_sem.at[1, i], device(z + way(yx, plane_peer(i)), plane_peer(i)),
        )

    def z_copy(g, h, half):
        rows = pl.ds(half * (HALF // 2), HALF // 2)
        lanes = pl.ds(pl.multiple_of(h * HALF, HALF), HALF)
        return remote(
            relay.at[g, rows, lanes], vals.at[1, g, rows, lanes],
            z_sem.at[0, g, h, half], z_sem.at[1, g, h, half], device(z + 7 * way(8 * half, yx), yx),
        )

    def v_copy(i, slot_at_receiver):
        return remote(
            vloc.at[plane_peer(i)], vals.at[0, :, rows_at(slot_at_receiver)],
            v_sem.at[0, i], v_sem.at[1, i], plane_device(i),
        )

    def g_copy(i, slot_at_receiver):
        return remote(
            gloc.at[plane_peer(i)], gpad.at[:, rows_at(slot_at_receiver)],
            g_sem.at[0, i], g_sem.at[1, i], plane_device(i),
        )

    tap_trade = remote(tap_own.at[1 - core], tap_sib, sib_sem.at[0, 0], sib_sem.at[1, 0], sibling)
    fg_trade = remote(fg_own.at[1 - core], fg_sib, sib_sem.at[0, 1], sib_sem.at[1, 1], sibling)

    def tap_copy(r, half, row):
        return remote(
            tap_mix.at[pile_peer(r) // 2], taps_in.at[half, row],
            tap_sem.at[0, r], tap_sem.at[1, r], pile_device(r),
        )

    def lo_copy(g, i, slot_at_receiver):
        return remote(
            lo.at[g, rows_at(plane_peer(i))], lo_in.at[slot_at_receiver, g],
            lo_sem.at[0, g, i], lo_sem.at[1, g, i], plane_device(i),
        )

    def fg_copy(r, row, half):
        peer = pile_peer(r)
        return remote(
            fg.at[lax.rem(peer, 2), peer // 2], fg_in.at[row, half],
            fg_sem.at[0, r], fg_sem.at[1, r], pile_device(r),
        )

    loop(0, N_SLOT, lambda i: r_copy(i, yx).start())
    tap_trade.start()
    loop(1, N_SLOT, lambda i: v_copy(i, yx).start())
    tap_trade.wait_recv()
    mine, other = tap_own[core], tap_sib[...]
    tap_mix[...] = jnp.concatenate(
        [jnp.where(core == 0, mine, other), jnp.where(core == 0, other, mine)], axis=1
    ).astype(BF16)
    loop(1, PILE, lambda r: tap_copy(r, side, z_lo).start())
    loop(1, N_SLOT, lambda i: g_copy(i, yx).start())

    for half in range(2):
        for n in range(8 * half, 8 * half + 8):
            r_copy(lax.rem(yx + N_SLOT - n, N_SLOT), n).wait_recv()
        z_copy(0, 0, half).start()
    for half in range(2):
        z_copy(0, 1, half).start()

    taps_in[side, z_lo] = tap_mix[z_lo]
    for g in range(2):
        gpad[g, rows_at(yx)] = gloc[yx, g]
        gpad[g, HALF:] = jnp.zeros((HALF, BLK), BF16)
        vals[0, g, rows_at(yx)] = vloc[yx, g]

    loads[4].wait()
    skip_rows[...] = jnp.broadcast_to(skip[...], (T, BLK)).T

    q_at = lax.broadcasted_iota(jnp.int32, (T, T), 0)
    p_at = lax.broadcasted_iota(jnp.int32, (T, T), 1)
    upper = p_at >= q_at

    for g in range(2):
        toep[g, :PAD] = jnp.zeros((PAD, T, T), BF16)
        for n in [0, 1, 2] + list(range(3, N_T + PAD, 8)) + list(range(N_T + 4, N_T + PAD + 1)):
            lags[g, n] = jnp.zeros((T, T), F32)

    loop(1, PILE, lambda r: tap_copy(r, lax.rem(pile_source(r), 2), pile_source(r) // 2).wait_recv())
    for g in range(2):

        def build(d, before, g=g):
            rows = taps_in[g, d].astype(F32)
            for c in range(16):
                turned = pltpu.roll(jnp.broadcast_to(rows[c : c + 1], (T, T)), 0, 1, stride=1, stride_axis=0)
                toep[g, PAD + d * 16 + c] = jnp.where(upper, turned, before).astype(BF16)
                before = turned
            return before

        lax.fori_loop(0, 8, build, jnp.zeros((T, T), F32))

    def convolve(half, g, h, width):
        lanes = pl.ds(pl.multiple_of(h * HALF, HALF), width * HALF)
        for d in range(N_SLOT):
            base = 8 * d + PAD if half == 0 else 8 * d + 8 * side - 4 - 2 * h + PAD
            left = vals[half, g, : HALF - d * GROUP, lanes]
            tiles = {n: toep[g, base + n] for n in range(1 - 2 * width, 4)}
            right = jnp.concatenate(
                [jnp.concatenate([tiles[v - u] for v in range(4)], axis=1) for u in range(2 * width)], axis=0
            )
            product = jnp.dot(left, right, preferred_element_type=F32)
            if half == 0 and d == 0:
                acc[g] = product
            else:
                acc[g, d * GROUP :] += product

    def correlate(half, g, h, width):
        lanes = pl.ds(pl.multiple_of(h * HALF, HALF), width * HALF)
        left = vals[half, g, :, lanes].T
        for d in range(N_SLOT):
            base = 8 * d + PAD if half == 0 else 8 * d + 8 * side - 4 - 2 * h + PAD
            right = gpad[g, d * GROUP : d * GROUP + HALF, :]
            product = jnp.dot(left, right, preferred_element_type=F32)
            for n in range(1 - 2 * width, 4):
                part = functools.reduce(
                    lambda a, b: a + b,
                    [
                        product[w * T : (w + 1) * T, (w + n) * T : (w + n + 1) * T]
                        for w in range(2 * width)
                        if 0 <= w + n < 4
                    ],
                )
                if half == 0:
                    lags[g, base + n] = part
                else:
                    lags[g, base + n] += part

    def finish_conv(g):
        scale = skip_rows[pl.ds(pl.multiple_of((yx * 2 + g) * GROUP, GROUP), GROUP), :]
        scale = jnp.concatenate([scale] * 4, axis=1)
        for n in range(N_SLOT):
            wide = vals[0, g, n * GROUP : (n + 1) * GROUP, :].astype(F32)
            rows = slice(n * GROUP, (n + 1) * GROUP)
            lo[g, rows, :] = (acc[g, rows, :] * (1.0 / 128.0) + scale * wide).astype(BF16)
        loop(1, N_SLOT, lambda i: lo_copy(g, i, yx).start())
        lo_in[yx, g] = lo[g, rows_at(yx), :]

    def finish_corr(g):
        def strip(d):
            for c in range(8):
                at = PAD + d * 8 + c
                mixed = jnp.where(upper, lags[g, at], lags[g, at + 1]).astype(BF16)
                diag[d * 8 + c] = functools.reduce(
                    lambda a, b: a + b,
                    [pltpu.roll(mixed[q : q + 16], (T - q) % T, 1).astype(F32) for q in range(0, T, 16)],
                )

        loop(0, N_DP, strip, False)
        total = functools.reduce(
            lambda a, b: a + b, [pltpu.roll(diag[:, q, :], (T - q) % T, 1) for q in range(16)]
        )
        fg[g] = total.reshape(8, 16, T).astype(BF16)

        def send(r):
            @pl.when(lax.rem(pile_peer(r), 2) == g)
            def _():
                fg_copy(r, z_lo, side).start()

        loop(1, PILE, send)

    def arrived(i):
        v_copy(i, plane_source(i)).wait_recv()
        g_copy(i, plane_source(i)).wait_recv()

    loop(1, N_SLOT, arrived)

    def own(g):
        convolve(0, g, 0, 2)
        correlate(0, g, 0, 2)

    loop(0, 2, own)

    def sent():
        def plane(i):
            v_copy(i, yx).wait_send()
            g_copy(i, yx).wait_send()

        loop(1, N_SLOT, plane)

        loop(0, N_SLOT, lambda i: r_copy(i, yx).wait_send())
        loop(1, PILE, lambda r: tap_copy(r, side, z_lo).wait_send())
        tap_trade.wait_send()

    def close_filter_grad():
        loop(1, PILE, lambda r: fg_copy(r, pile_source(r) // 2, lax.rem(pile_source(r), 2)).wait_recv())
        fg_in[z_lo, side] = fg[side, z_lo]
        both = (fg_in[:, 0].astype(F32) + fg_in[:, 1].astype(F32)) * (1.0 / 512.0)
        fg_own[0] = both[:, :8]
        fg_own[1] = both[:, 8:]
        fg_trade.start()
        fg_trade.wait_recv()
        mine, other = fg_own[core], fg_sib[...]
        fg_rows[:, 0] = jnp.where(core == 0, mine, other)
        fg_rows[:, 1] = jnp.where(core == 0, other, mine)
        for b in range(N_DP):
            for c in range(8):
                fg_ref[b : b + 1, c * T : (c + 1) * T] = fg_rows[b // 2, b % 2, c : c + 1, :]

    def phase(n):
        g = n // 2
        h = lax.rem(n, 2)
        pl.when(n == 3)(sent)
        for half in range(2):
            z_copy(g, h, half).wait_recv()

        @pl.when(n == 0)
        def _():
            for half in range(2):
                z_copy(1, 0, half).start()

        convolve(1, g, h, 1)

        @pl.when(h == 1)
        def _():
            finish_conv(g)

        correlate(1, g, h, 1)

        @pl.when(h == 1)
        def _():
            finish_corr(g)

        @pl.when(n == 1)
        def _():
            for half in range(2):
                z_copy(1, 1, half).start()

    loop(0, 4, phase)
    pl.when(side == 0)(close_filter_grad)

    for g in range(2):
        loop(1, N_SLOT, lambda i, g=g: lo_copy(g, i, plane_source(i)).wait_recv())
    out_ref[...] = lo_in[...].reshape(BLK, BLK).T

    pl.when(side == 1)(close_filter_grad)
    fg_trade.wait_send()
    for g in range(2):
        for h in range(2):
            for half in range(2):
                z_copy(g, h, half).wait_send()
    for g in range(2):
        loop(1, N_SLOT, lambda i, g=g: lo_copy(g, i, yx).wait_send())
    loop(1, PILE, lambda r: fg_copy(r, z_lo, side).wait_send())


def shards(value, gate, grad_out, filter_taps, skip):
    taps = filter_taps[:, 0, :].T
    any_spec = pl.BlockSpec(memory_space=pl.ANY)
    vmem_spec = pl.BlockSpec(memory_space=pltpu.VMEM)
    long_out, fg = pl.pallas_call(
        kernel,
        out_shape=(
            jax.ShapeDtypeStruct((BLK, BLK), BF16),
            jax.ShapeDtypeStruct((N_DP, 1024), F32),
        ),
        in_specs=[any_spec] * 5,
        out_specs=(vmem_spec, vmem_spec),
        scratch_shapes=[
            pltpu.VMEM((BLK, BLK), BF16),
            pltpu.VMEM((BLK, BLK), BF16),
            pltpu.VMEM((BLK, BLK), BF16),
            pltpu.VMEM((N_DP, 1024), F32),
            pltpu.VMEM((1, BLK), F32),
            pltpu.VMEM((BLK, T), F32),
            pltpu.VMEM((N_SLOT, 2, GROUP, BLK), BF16),
            pltpu.VMEM((N_SLOT, 2, GROUP, BLK), BF16),
            pltpu.VMEM((2, 8, 8, T), F32),
            pltpu.VMEM((8, 8, T), F32),
            pltpu.VMEM((8, 16, T), BF16),
            pltpu.VMEM((2, 8, 16, T), BF16),
            pltpu.VMEM((2, N_T + PAD, T, T), BF16),
            pltpu.VMEM((2, HALF, BLK), BF16),
            pltpu.VMEM((2, 2, HALF, BLK), BF16),
            pltpu.VMEM((2, BLK, BLK), BF16),
            pltpu.VMEM((2, HALF, BLK), F32),
            pltpu.VMEM((2, N_T + PAD + 1, T, T), F32),
            pltpu.VMEM((N_T, 16, T), F32),
            pltpu.VMEM((2, HALF, BLK), BF16),
            pltpu.VMEM((N_SLOT, 2, GROUP, BLK), BF16),
            pltpu.VMEM((2, 8, 16, T), BF16),
            pltpu.VMEM((8, 2, 16, T), BF16),
            pltpu.VMEM((2, 8, 8, T), F32),
            pltpu.VMEM((8, 8, T), F32),
            pltpu.VMEM((8, 2, 8, T), F32),
            pltpu.SemaphoreType.DMA((5,)),
            pltpu.SemaphoreType.DMA((2, N_SLOT)),
            pltpu.SemaphoreType.DMA((2, N_SLOT)),
            pltpu.SemaphoreType.DMA((2, N_SLOT)),
            pltpu.SemaphoreType.DMA((2, 2, 2, 2)),
            pltpu.SemaphoreType.DMA((2, PILE)),
            pltpu.SemaphoreType.DMA((2, 2, N_SLOT)),
            pltpu.SemaphoreType.DMA((2, PILE)),
            pltpu.SemaphoreType.DMA((2, 2)),
        ],
        compiler_params=pltpu.CompilerParams(
            collective_id=0, has_side_effects=True, vmem_limit_bytes=56 * 2**20
        ),
        cost_estimate=pl.CostEstimate(flops=2 * 2**33, bytes_accessed=4 * 2**20, transcendentals=0),
        name="hyena",
    )(value, gate, grad_out, taps, skip[None, :])
    grad = (long_out.astype(F32) * grad_out.astype(F32)).astype(BF16)
    return grad, fg.T[:, None, :]


def solution(mesh):
    in_specs = (P("ctx", "dp"), P("ctx", "dp"), P("ctx", "dp"), P("dp", "ctx", None), P("dp"))
    out_specs = (P("ctx", "dp"), P("dp", "ctx", None))
    return jax.shard_map(shards, mesh=mesh, in_specs=in_specs, out_specs=out_specs, check_vma=False)
```

```python
import functools

import jax
import jax.numpy as jnp
from jax import lax
from jax.experimental import pallas as pl
from jax.experimental.pallas import tpu as pltpu
from jax.sharding import PartitionSpec as P

MESH = pl.DeviceIdType.MESH
BF16 = jnp.bfloat16
F32 = jnp.float32

N_DP = 16
N_SLOT = 16
GROUP = 16
BLK = 512
T = 128
HALF = 256
PAD = 7
N_T = 128
PILE = 16


def remote(src, dst, send, recv, device):
    return pltpu.make_async_remote_copy(
        src_ref=src, dst_ref=dst, send_sem=send, recv_sem=recv, device_id=device, device_id_type=MESH
    )


def loop(lower, upper, body, unroll=True):
    def step(i, carry):
        body(i)
        return carry

    if upper - lower in (15, 16) and unroll:
        for i in range(lower, upper):
            body(i)
        return
    lax.fori_loop(lower, upper, step, 0)


def kernel(
    value_hbm, gate_hbm, cot_hbm, taps_hbm, skip_hbm,
    out_ref, fg_ref,
    val, gat, cot, taps, skip, skip_rows,
    vloc, gloc, tap_own, tap_sib, tap_mix, taps_in, toep, relay, vals, gpad, acc, lags, diag, lo, lo_in,
    fg, fg_in, fg_own, fg_sib, fg_rows,
    in_sem, v_sem, g_sem, r_sem, z_sem, tap_sem, lo_sem, fg_sem, sib_sem,
):
    dp = lax.axis_index("dp")
    ctx = lax.axis_index("ctx")
    core = lax.rem(dp, 2)
    side = lax.rem(ctx, 2)
    yx = ctx // 2
    z = side * 8 + dp // 2
    z_lo = dp // 2
    pile = z_lo * 2 + side
    sibling = (dp + 1 - 2 * core, ctx)

    def device(z_at, yx_at):
        z_at = lax.rem(z_at + 16, 16)
        return (lax.rem(z_at, 8) * 2 + core, yx_at * 2 + z_at // 8)

    def plane_peer(i):
        return lax.rem(yx + i, N_SLOT)

    def plane_device(i):
        return (dp, plane_peer(i) * 2 + side)

    def plane_source(i):
        return lax.rem(yx + N_SLOT - i, N_SLOT)

    def pile_peer(r):
        return lax.rem(pile + r, PILE)

    def pile_device(r):
        peer = pile_peer(r)
        return (peer // 2 * 2 + core, yx * 2 + lax.rem(peer, 2))

    def pile_source(r):
        return lax.rem(pile + PILE - r, PILE)

    def way(one, two):
        return 1 - 2 * lax.rem(one // 8 + two // 8, 2)

    def rows_at(slot):
        return pl.ds(pl.multiple_of(slot * GROUP, GROUP), GROUP)

    barrier = pltpu.get_barrier_semaphore()

    def greet(target):
        pl.semaphore_signal(barrier, inc=1, device_id=target, device_id_type=MESH)

    loop(1, PILE, lambda r: greet(pile_device(r)))
    greet(sibling)
    loop(1, N_SLOT, lambda i: greet(device(z - way(plane_source(i), yx), plane_source(i))))
    loop(1, N_SLOT, lambda i: greet(plane_device(i)))

    loads = [
        pltpu.make_async_copy(src, dst, in_sem.at[n])
        for n, (src, dst) in enumerate(
            ((value_hbm, val), (taps_hbm, taps), (cot_hbm, cot), (gate_hbm, gat), (skip_hbm, skip))
        )
    ]
    for load in loads:
        load.start()

    loads[0].wait()
    vloc[...] = val[...].T.reshape(N_SLOT, 2, GROUP, BLK)
    loads[1].wait()
    for b in range(N_DP):
        for c in range(8):
            tap_own[b % 2, b // 2, c : c + 1, :] = taps[b : b + 1, c * T : (c + 1) * T]
    loads[2].wait()
    loads[3].wait()
    gloc[...] = (gat[...].astype(F32) * cot[...].astype(F32)).astype(BF16).T.reshape(N_SLOT, 2, GROUP, BLK)

    @pl.when(side == 0)
    def _():
        for g in range(2):
            vals[1, g, HALF - GROUP :] = jnp.zeros((GROUP, BLK), BF16)

    pl.semaphore_wait(barrier, PILE + 2 * (N_SLOT - 1))

    def r_copy(i, slot_at_receiver):
        return remote(
            vloc.at[plane_peer(i)], relay.at[:, rows_at(slot_at_receiver)],
            r_sem.at[0, i], r_sem.at[1, i], device(z + way(yx, plane_peer(i)), plane_peer(i)),
        )

    def z_copy(g, h, half, short=False):
        rows = pl.ds(half * (HALF // 2), HALF // 2 - GROUP if short else HALF // 2)
        lanes = pl.ds(pl.multiple_of(h * HALF, HALF), HALF)
        return remote(
            relay.at[g, rows, lanes], vals.at[1, g, rows, lanes],
            z_sem.at[0, g, h, half], z_sem.at[1, g, h, half], device(z + 7 * way(8 * half, yx), yx),
        )

    def z_each(g, h, half, to_side, act):
        if half == 0:
            act(z_copy(g, h, 0))
        else:
            pl.when(to_side == 0)(lambda: act(z_copy(g, h, 1, True)))
            pl.when(to_side == 1)(lambda: act(z_copy(g, h, 1)))

    late_side = lax.rem(z + 7 * way(8, yx) + 16, 16) // 8

    def z_start(g, h, half):
        z_each(g, h, half, late_side, lambda copy: copy.start())

    def z_wait_send(g, h, half):
        z_each(g, h, half, late_side, lambda copy: copy.wait_send())

    def z_wait_recv(g, h, half):
        z_each(g, h, half, side, lambda copy: copy.wait_recv())

    def v_copy(i, slot_at_receiver):
        return remote(
            vloc.at[plane_peer(i)], vals.at[0, :, rows_at(slot_at_receiver)],
            v_sem.at[0, i], v_sem.at[1, i], plane_device(i),
        )

    def g_copy(i, slot_at_receiver):
        return remote(
            gloc.at[plane_peer(i)], gpad.at[:, rows_at(slot_at_receiver)],
            g_sem.at[0, i], g_sem.at[1, i], plane_device(i),
        )

    tap_trade = remote(tap_own.at[1 - core], tap_sib, sib_sem.at[0, 0], sib_sem.at[1, 0], sibling)
    fg_trade = remote(fg_own.at[1 - core], fg_sib, sib_sem.at[0, 1], sib_sem.at[1, 1], sibling)

    def tap_copy(r, half, row):
        return remote(
            tap_mix.at[pile_peer(r) // 2], taps_in.at[half, row],
            tap_sem.at[0, r], tap_sem.at[1, r], pile_device(r),
        )

    def lo_copy(g, i, slot_at_receiver):
        return remote(
            lo.at[g, rows_at(plane_peer(i))], lo_in.at[slot_at_receiver, g],
            lo_sem.at[0, g, i], lo_sem.at[1, g, i], plane_device(i),
        )

    def fg_copy(r, row, half):
        peer = pile_peer(r)
        return remote(
            fg.at[lax.rem(peer, 2), peer // 2], fg_in.at[row, half],
            fg_sem.at[0, r], fg_sem.at[1, r], pile_device(r),
        )

    loop(0, N_SLOT, lambda i: r_copy(i, yx).start())
    tap_trade.start()
    loop(1, N_SLOT, lambda i: v_copy(i, yx).start())
    tap_trade.wait_recv()
    mine, other = tap_own[core], tap_sib[...]
    tap_mix[...] = jnp.concatenate(
        [jnp.where(core == 0, mine, other), jnp.where(core == 0, other, mine)], axis=1
    ).astype(BF16)
    loop(1, PILE, lambda r: tap_copy(r, side, z_lo).start())
    loop(1, N_SLOT, lambda i: g_copy(i, yx).start())

    for half in range(2):
        for n in range(8 * half, 8 * half + 8):
            r_copy(lax.rem(yx + N_SLOT - n, N_SLOT), n).wait_recv()
        z_start(0, 0, half)
    for half in range(2):
        z_start(0, 1, half)

    taps_in[side, z_lo] = tap_mix[z_lo]
    for g in range(2):
        gpad[g, rows_at(yx)] = gloc[yx, g]
        gpad[g, HALF:] = jnp.zeros((HALF, BLK), BF16)
        vals[0, g, rows_at(yx)] = vloc[yx, g]

    loads[4].wait()
    skip_rows[...] = jnp.broadcast_to(skip[...], (T, BLK)).T

    q_at = lax.broadcasted_iota(jnp.int32, (T, T), 0)
    p_at = lax.broadcasted_iota(jnp.int32, (T, T), 1)
    upper = p_at >= q_at

    for g in range(2):
        toep[g, :PAD] = jnp.zeros((PAD, T, T), BF16)
        for n in [0, 1, 2] + list(range(3, N_T + PAD, 8)) + list(range(N_T + 4, N_T + PAD + 1)):
            lags[g, n] = jnp.zeros((T, T), F32)

    loop(1, PILE, lambda r: tap_copy(r, lax.rem(pile_source(r), 2), pile_source(r) // 2).wait_recv())
    for g in range(2):

        def build(d, before, g=g):
            rows = taps_in[g, d].astype(F32)
            for c in range(16):
                turned = pltpu.roll(jnp.broadcast_to(rows[c : c + 1], (T, T)), 0, 1, stride=1, stride_axis=0)
                toep[g, PAD + d * 16 + c] = jnp.where(upper, turned, before).astype(BF16)
                before = turned
            return before

        lax.fori_loop(0, 8, build, jnp.zeros((T, T), F32))

    def convolve(half, g, h, width):
        lanes = pl.ds(pl.multiple_of(h * HALF, HALF), width * HALF)
        for d in range(N_SLOT):
            base = 8 * d + PAD if half == 0 else 8 * d + 8 * side - 4 - 2 * h + PAD
            left = vals[half, g, : HALF - d * GROUP, lanes]
            tiles = {n: toep[g, base + n] for n in range(1 - 2 * width, 4)}
            right = jnp.concatenate(
                [jnp.concatenate([tiles[v - u] for v in range(4)], axis=1) for u in range(2 * width)], axis=0
            )
            product = jnp.dot(left, right, preferred_element_type=F32)
            if half == 0 and d == 0:
                acc[g] = product
            else:
                acc[g, d * GROUP :] += product

    def correlate(half, g, h, width):
        lanes = pl.ds(pl.multiple_of(h * HALF, HALF), width * HALF)
        left = vals[half, g, :, lanes].T
        for d in range(N_SLOT):
            base = 8 * d + PAD if half == 0 else 8 * d + 8 * side - 4 - 2 * h + PAD
            right = gpad[g, d * GROUP : d * GROUP + HALF, :]
            product = jnp.dot(left, right, preferred_element_type=F32)
            for n in range(1 - 2 * width, 4):
                part = functools.reduce(
                    lambda a, b: a + b,
                    [
                        product[w * T : (w + 1) * T, (w + n) * T : (w + n + 1) * T]
                        for w in range(2 * width)
                        if 0 <= w + n < 4
                    ],
                )
                if half == 0:
                    lags[g, base + n] = part
                else:
                    lags[g, base + n] += part

    def finish_conv(g):
        scale = skip_rows[pl.ds(pl.multiple_of((yx * 2 + g) * GROUP, GROUP), GROUP), :]
        scale = jnp.concatenate([scale] * 4, axis=1)

        def piece(i):
            rows = rows_at(plane_peer(i))
            wide = vals[0, g, rows, :].astype(F32)
            return (acc[g, rows, :] * (1.0 / 128.0) + scale * wide).astype(BF16)

        def piece_out(i):
            lo[g, rows_at(plane_peer(i)), :] = piece(i)
            lo_copy(g, i, yx).start()

        loop(1, N_SLOT, piece_out)
        lo_in[yx, g] = piece(0)

    def finish_corr(g):
        def strip(d):
            for c in range(8):
                at = PAD + d * 8 + c
                mixed = jnp.where(upper, lags[g, at], lags[g, at + 1]).astype(BF16)
                diag[d * 8 + c] = functools.reduce(
                    lambda a, b: a + b,
                    [pltpu.roll(mixed[q : q + 16], (T - q) % T, 1).astype(F32) for q in range(0, T, 16)],
                )

        loop(0, N_DP, strip, False)
        total = functools.reduce(
            lambda a, b: a + b, [pltpu.roll(diag[:, q, :], (T - q) % T, 1) for q in range(16)]
        )
        fg[g] = total.reshape(8, 16, T).astype(BF16)

        def send(r):
            @pl.when(lax.rem(pile_peer(r), 2) == g)
            def _():
                fg_copy(r, z_lo, side).start()

        loop(1, PILE, send)

    def arrived(i):
        v_copy(i, plane_source(i)).wait_recv()
        g_copy(i, plane_source(i)).wait_recv()

    loop(1, N_SLOT, arrived)

    def own(g):
        convolve(0, g, 0, 2)
        correlate(0, g, 0, 2)

    loop(0, 2, own)

    def sent():
        def plane(i):
            v_copy(i, yx).wait_send()
            g_copy(i, yx).wait_send()

        loop(1, N_SLOT, plane)

        loop(0, N_SLOT, lambda i: r_copy(i, yx).wait_send())
        loop(1, PILE, lambda r: tap_copy(r, side, z_lo).wait_send())
        tap_trade.wait_send()

    def close_filter_grad():
        loop(1, PILE, lambda r: fg_copy(r, pile_source(r) // 2, lax.rem(pile_source(r), 2)).wait_recv())
        fg_in[z_lo, side] = fg[side, z_lo]
        both = (fg_in[:, 0].astype(F32) + fg_in[:, 1].astype(F32)) * (1.0 / 512.0)
        fg_own[0] = both[:, :8]
        fg_own[1] = both[:, 8:]
        fg_trade.start()
        fg_trade.wait_recv()
        mine, other = fg_own[core], fg_sib[...]
        fg_rows[:, 0] = jnp.where(core == 0, mine, other)
        fg_rows[:, 1] = jnp.where(core == 0, other, mine)
        for b in range(N_DP):
            for c in range(8):
                fg_ref[b : b + 1, c * T : (c + 1) * T] = fg_rows[b // 2, b % 2, c : c + 1, :]

    def phase(n):
        g = n // 2
        h = lax.rem(n, 2)
        pl.when(n == 3)(sent)
        for half in range(2):
            z_wait_recv(g, h, half)

        @pl.when(g == 0)
        def _():
            for half in range(2):
                z_start(1, h, half)

        convolve(1, g, h, 1)

        @pl.when(h == 1)
        def _():
            finish_conv(g)

        correlate(1, g, h, 1)

        @pl.when(h == 1)
        def _():
            finish_corr(g)

    loop(0, 4, phase)

    for g in range(2):
        loop(1, N_SLOT, lambda i, g=g: lo_copy(g, i, plane_source(i)).wait_recv())
    out_ref[...] = lo_in[...].reshape(BLK, BLK).T

    close_filter_grad()
    fg_trade.wait_send()
    for g in range(2):
        for h in range(2):
            for half in range(2):
                z_wait_send(g, h, half)
    for g in range(2):
        loop(1, N_SLOT, lambda i, g=g: lo_copy(g, i, yx).wait_send())
    loop(1, PILE, lambda r: fg_copy(r, z_lo, side).wait_send())


def shards(value, gate, grad_out, filter_taps, skip):
    taps = filter_taps[:, 0, :].T
    any_spec = pl.BlockSpec(memory_space=pl.ANY)
    vmem_spec = pl.BlockSpec(memory_space=pltpu.VMEM)
    long_out, fg = pl.pallas_call(
        kernel,
        out_shape=(
            jax.ShapeDtypeStruct((BLK, BLK), BF16),
            jax.ShapeDtypeStruct((N_DP, 1024), F32),
        ),
        in_specs=[any_spec] * 5,
        out_specs=(vmem_spec, vmem_spec),
        scratch_shapes=[
            pltpu.VMEM((BLK, BLK), BF16),
            pltpu.VMEM((BLK, BLK), BF16),
            pltpu.VMEM((BLK, BLK), BF16),
            pltpu.VMEM((N_DP, 1024), F32),
            pltpu.VMEM((1, BLK), F32),
            pltpu.VMEM((BLK, T), F32),
            pltpu.VMEM((N_SLOT, 2, GROUP, BLK), BF16),
            pltpu.VMEM((N_SLOT, 2, GROUP, BLK), BF16),
            pltpu.VMEM((2, 8, 8, T), F32),
            pltpu.VMEM((8, 8, T), F32),
            pltpu.VMEM((8, 16, T), BF16),
            pltpu.VMEM((2, 8, 16, T), BF16),
            pltpu.VMEM((2, N_T + PAD, T, T), BF16),
            pltpu.VMEM((2, HALF, BLK), BF16),
            pltpu.VMEM((2, 2, HALF, BLK), BF16),
            pltpu.VMEM((2, BLK, BLK), BF16),
            pltpu.VMEM((2, HALF, BLK), F32),
            pltpu.VMEM((2, N_T + PAD + 1, T, T), F32),
            pltpu.VMEM((N_T, 16, T), F32),
            pltpu.VMEM((2, HALF, BLK), BF16),
            pltpu.VMEM((N_SLOT, 2, GROUP, BLK), BF16),
            pltpu.VMEM((2, 8, 16, T), BF16),
            pltpu.VMEM((8, 2, 16, T), BF16),
            pltpu.VMEM((2, 8, 8, T), F32),
            pltpu.VMEM((8, 8, T), F32),
            pltpu.VMEM((8, 2, 8, T), F32),
            pltpu.SemaphoreType.DMA((5,)),
            pltpu.SemaphoreType.DMA((2, N_SLOT)),
            pltpu.SemaphoreType.DMA((2, N_SLOT)),
            pltpu.SemaphoreType.DMA((2, N_SLOT)),
            pltpu.SemaphoreType.DMA((2, 2, 2, 2)),
            pltpu.SemaphoreType.DMA((2, PILE)),
            pltpu.SemaphoreType.DMA((2, 2, N_SLOT)),
            pltpu.SemaphoreType.DMA((2, PILE)),
            pltpu.SemaphoreType.DMA((2, 2)),
        ],
        compiler_params=pltpu.CompilerParams(
            collective_id=0, has_side_effects=True, vmem_limit_bytes=56 * 2**20
        ),
        cost_estimate=pl.CostEstimate(flops=2 * 2**33, bytes_accessed=4 * 2**20, transcendentals=0),
        name="hyena",
    )(value, gate, grad_out, taps, skip[None, :])
    grad = (long_out.astype(F32) * grad_out.astype(F32)).astype(BF16)
    return grad, fg.T[:, None, :]


def solution(mesh):
    in_specs = (P("ctx", "dp"), P("ctx", "dp"), P("ctx", "dp"), P("dp", "ctx", None), P("dp"))
    out_specs = (P("ctx", "dp"), P("dp", "ctx", None))
    return jax.shard_map(shards, mesh=mesh, in_specs=in_specs, out_specs=out_specs, check_vma=False)
```
